32 devices in a mesh: tile: 8 (over z, core), offs: 4 (over y, x).
Axes of the slice: x: 2, y: 2, z: 4, core: 2. Of those that a mesh axis runs over, the one named last changes fastest.
Arguments:
- traces: float32 [4, 64, 2, 2000], P('offs', 'tile'), may hold values from -6 to 6
- src_node: int32 [4, 64], P('offs', 'tile'), may hold values from 0 to 31
- rec_node: int32 [4, 64, 2], P('offs', 'tile'), may hold values from 0 to 31
- aperture: int32 [4, 64, 2], P('offs', 'tile'), may hold values from 0 to 7, all different within a row; in each aligned block of 8 rows (0 to 7, 8 to 15, ..., all dimensions but the last counted through in order) at most 3 rows name the same one
- time_table: int32 [32, 8, 2048], P(None, 'tile'), may hold values from 0 to 999
- amp_table: float32 [32, 8, 2048], P(None, 'tile'), may hold values from 0.05 to 0.5
- width_table: int32 [32, 8, 2048], P(None, 'tile'), may hold values from 0 to 2
Outputs:
- gathers: float32 [8, 16, 4, 128], P('tile', 'offs')
The draws below stay inside these ranges and needn't reach their ends.
Inputs may be any that keep to these rules, and one draw needn't show every extreme that they name: `aperture`: each row names 2 different image tiles. Among the 8 rows of one device (aligned blocks of rows in the order offset class, block), no tile is named more than 3 times, a bound that some block reaches.
All inputs are finite; a program needn't handle non-finite values.
Results may differ from the reference program's by a relative error of at most 0.0003.
Values sent between devices are 32-bit elements; how exact they have to be, the bound alone decides.
No kernel may reach another device: no remote copies, remote signals or barrier semaphores. Data moves between devices by JAX's collectives and lax.ppermute only.
A program may use at most 64 MiB of HBM per device.

```python
import math
import jax
import jax.numpy as jnp
import numpy as np
from jax import lax

NT = 2000
TB = 2
BLK_DEV = 8
APER = 2
NODES = 32
CELLS = 128
DEPTH = 16
CAP = 3
NTILE = 8
NOFF = 4
BT = 64
PTS = 2048


def place_ends(values, rng, least, high):
    longest = values.shape.index(max(values.shape))
    spots = []
    for shift in (0, 1):
        where = [jax.random.randint(jax.random.fold_in(rng, axis), (), 0, length) for axis, length in enumerate(values.shape)]
        where[longest] = (where[longest] + shift) % values.shape[longest]
        spots.append(tuple(where))
    return values.at[spots[0]].set(least).at[spots[1]].set(high)


def levels(rng, shape, cuts, least, top_value):
    gain = 1.0
    for position, blocks in cuts:
        draws = jax.random.uniform(jax.random.fold_in(jax.random.fold_in(rng, 6), position), (blocks,), jnp.float32, least / len(cuts), top_value / len(cuts))
        gain = gain * jnp.repeat(jnp.exp(draws), shape[position] // blocks).reshape((-1,) + (1,) * (len(shape) - 1 - position))
    return gain


def routed_block(rng, own, number, rows, number_of, top, most, skew):
    sequence = jax.random.permutation(rng, number_of)
    crowded, common = shares(number_of, rows * top, most, skew, True), shares(number_of, rows * top, most, skew, False)
    places = jnp.arange(number_of)

    def named(tallies, offset_by):
        used = int((tallies > 0).sum())
        fixed = max(1, used // 4)
        shifted = fixed + (places - fixed + offset_by * (used - fixed)) % max(1, number_of - fixed)
        return jnp.zeros((number_of,), jnp.int32).at[sequence[jnp.where(places < fixed, places, shifted)]].set(jnp.asarray(tallies, jnp.int32))

    tallies = jnp.where(number % 4 == 0, named(crowded, number // 4), named(common, number - number // 4 - 1))
    mixed = jax.random.permutation(jax.random.fold_in(own, 3), number_of)
    source_of, sink = mixed[0:number_of // 2 * 2:2], mixed[1:number_of // 2 * 2:2]
    margin = jnp.minimum(tallies[source_of] - 1, most - tallies[sink]) // 2
    margin = jnp.where((source_of == sequence[0]) | (sink == sequence[0]) | (tallies[sink] == 0), 0, jnp.maximum(margin, 0))
    shifted = jax.random.randint(jax.random.fold_in(own, 4), (number_of // 2,), 0, 1 << 20) % (margin + 1)
    tallies = tallies.at[source_of].add(-shifted).at[sink].add(shifted)
    items = jnp.searchsorted(jnp.cumsum(tallies), jnp.arange(rows * top), side="right").astype(jnp.int32)
    table = items.reshape(top, rows).T
    table = table[jax.random.permutation(jax.random.fold_in(own, 1), rows)]
    offset_by = jax.random.randint(jax.random.fold_in(own, 2), (rows, 1), 0, top)
    return jnp.take_along_axis(table, (jnp.arange(top)[None, :] + offset_by) % top, axis=1)


def shares(amount, total, bound, slope, full):
    portions = [(1 << 20) // math.isqrt(rank ** slope) + 1 for rank in range(1, amount + 1)]
    largest = bound if full else min(bound, max(-(-total // amount), total * portions[0] // sum(portions)))
    least = 1 if total - largest >= amount - 1 else 0
    given, surplus = [largest] + [least] * (amount - 1), total - largest - least * (amount - 1)
    while surplus > 0:
        movable = [i for i in range(1, amount) if given[i] < largest] or [i for i in range(1, amount) if given[i] < bound]
        whole, left = sum([portions[i] for i in movable]), surplus
        for i in movable:
            extra = min(bound - given[i], max(1, left * portions[i] // whole), surplus)
            given[i] = given[i] + extra
            surplus = surplus - extra
    return np.array(given)


def gaussian(stream_key, dims, scale, most, split=(), held_as=jnp.bfloat16):
    array = jax.random.normal(stream_key, dims, jnp.float32) * scale
    if len(split) > 0:
        array = levels(stream_key, dims, split, -0.22, 0.18) * array
    return jnp.clip(array, min=-most, max=most).astype(held_as)


def setup_inputs(seed: int = 0) -> dict:
    seeds = jax.random.split(jax.random.key(seed), 8)
    traces = gaussian(seeds[0], (NOFF, BT, TB, NT), 1.0, 6.0, ((0, 4), (1, 8)), jnp.float32)
    src_node = place_ends(jax.random.randint(seeds[1], (NOFF, BT), 0, NODES), jax.random.fold_in(seeds[1], 1), 0, NODES - 1).astype(jnp.int32)
    rec_node = place_ends(jax.random.randint(seeds[2], (NOFF, BT, TB), 0, NODES), jax.random.fold_in(seeds[2], 1), 0, NODES - 1).astype(jnp.int32)
    aperture_keys = jax.random.split(jax.random.fold_in(seeds[3], 1), NOFF * BT // BLK_DEV)
    aperture_turns = jax.random.permutation(jax.random.fold_in(seeds[3], 3), NOFF * BT // BLK_DEV)
    aperture = jax.vmap(lambda own, number: routed_block(jax.random.fold_in(seeds[3], 2), own, number, BLK_DEV, NTILE, APER, CAP, 2))(aperture_keys, aperture_turns).reshape((NOFF, BT, APER))
    time_table = place_ends(jax.random.randint(seeds[4], (NODES, NTILE, PTS), 0, NT // 2), jax.random.fold_in(seeds[4], 1), 0, (NT // 2) - 1).astype(jnp.int32)
    amp_table = jnp.clip(jnp.exp(math.log(0.5) - 2.3025851 * jax.random.uniform(seeds[5], (NODES, NTILE, PTS), jnp.float32) ** levels(seeds[5], (NODES, NTILE, PTS), ((1, 8),), -0.2, 0.2)), 0.05, 0.5)
    width_table = place_ends(jax.random.randint(seeds[6], (NODES, NTILE, PTS), 0, 3), jax.random.fold_in(seeds[6], 1), 0, 2).astype(jnp.int32)
    return dict(traces=traces, src_node=src_node, rec_node=rec_node, aperture=aperture, time_table=time_table, amp_table=amp_table, width_table=width_table)


HALF_WIDTHS = (1, 2, 4)


def triangle(signal):
    length = signal.shape[-1]
    last_axis = signal.ndim - 1
    layers = []
    for halfwidth in HALF_WIDTHS:
        padded = jnp.pad(signal, [(0, 0)] * last_axis + [(halfwidth, halfwidth)])
        summed = jnp.zeros(signal.shape, signal.dtype)
        for offset in range(-halfwidth, halfwidth + 1):
            factor = float(halfwidth + 1 - abs(offset)) / float((halfwidth + 1) ** 2)
            summed = summed + factor * lax.slice_in_dim(padded, halfwidth + offset, halfwidth + offset + length, axis=last_axis)
        layers.append(summed)
    return jnp.stack(layers, axis=-2)


def spread(filtered, sources, receivers, live, time_rows, amp_rows, width_rows):
    samples = filtered.shape[-1]
    source_time = jnp.take(time_rows, sources, axis=0)[:, None, :]
    index_time = source_time + jnp.take(time_rows, receivers, axis=0)
    width_class = jnp.maximum(jnp.take(width_rows, sources, axis=0)[:, None, :], jnp.take(width_rows, receivers, axis=0))
    weight = jnp.take(amp_rows, sources, axis=0)[:, None, :] * jnp.take(amp_rows, receivers, axis=0) * live[:, None, None]
    flat = filtered.reshape(filtered.shape[0] * filtered.shape[1], -1)
    column = (width_class * samples + index_time).reshape(flat.shape[0], -1).astype(jnp.int32)
    picked = jnp.take_along_axis(flat, column, axis=1)
    return jnp.sum(weight.reshape(picked.shape) * picked, axis=0)


def reference(traces, src_node, rec_node, aperture, time_table, amp_table, width_table):
    classes = traces.shape[0]
    blocks = traces.shape[1]
    points = time_table.shape[2]
    image = jnp.zeros((classes, NTILE, points), traces.dtype)
    signals = traces.reshape(classes * blocks, TB, NT)
    sources = src_node.reshape(classes * blocks)
    receivers = rec_node.reshape(classes * blocks, TB)
    targets = aperture.reshape(classes * blocks, APER)
    row_ids = jnp.arange(classes * blocks, dtype=jnp.int32)

    def advance(image, inputs):
        signal, source, receiver_ids, target_ids, row = inputs
        filtered = triangle(signal)[None]
        offset_class = (row // blocks).astype(jnp.int32)
        ones = jnp.ones((1,), traces.dtype)
        for entry in range(APER):
            target = target_ids[entry].astype(jnp.int32)
            time_rows = lax.dynamic_index_in_dim(time_table, target, axis=1, keepdims=False)
            amp_rows = lax.dynamic_index_in_dim(amp_table, target, axis=1, keepdims=False)
            width_rows = lax.dynamic_index_in_dim(width_table, target, axis=1, keepdims=False)
            contribution = spread(filtered, source[None], receiver_ids[None], ones, time_rows, amp_rows, width_rows)
            current = lax.dynamic_slice(image, (offset_class, target, jnp.int32(0)), (1, 1, points))
            image = lax.dynamic_update_slice(image, current + contribution[None, None], (offset_class, target, jnp.int32(0)))
        return image, None

    image, _ = lax.scan(advance, image, (signals, sources, receivers, targets, row_ids))
    return image.reshape(classes, NTILE, DEPTH, CELLS).transpose(1, 2, 0, 3)
```

```python
import functools

import jax
import jax.numpy as jnp
from jax import lax
from jax.experimental import pallas as pl
from jax.experimental.pallas import tpu as pltpu
from jax.sharding import PartitionSpec as P

LANES = 128
SUBLANES = 8
VMEM = pl.BlockSpec(memory_space=pltpu.VMEM)
SMEM = pl.BlockSpec(memory_space=pltpu.SMEM)
PARAMS = pltpu.CompilerParams(vmem_limit_bytes=24 << 20)


def pack_kernel(chips, capacity, src, rec, ap, traces, *rest):
    outs, block_of, count = rest[:-2], rest[-2], rest[-1]
    blocks, per_block, samples = traces.shape[1:]
    listed = ap.shape[0]
    me = lax.axis_index("tile")
    z, core = me >> 1, me & 1
    for n in range(2 * chips):
        count[n] = 0
    for n in range(2 * chips * capacity):
        block_of[n] = -1
    for b in range(blocks):
        for e in range(listed):
            tile = ap[e, b]
            group = ((tile >> 1) ^ z) * 2 + ((tile & 1) ^ core)
            place = count[group]
            count[group] = place + 1
            block_of[group * capacity + place] = b
    full, tail = samples // LANES, samples % LANES
    lane = lax.broadcasted_iota(jnp.int32, (per_block, LANES), 1)
    for k in range(chips):
        for slot in range(2 * capacity):
            b = block_of[k * 2 * capacity + slot]
            live = b >= 0
            b = jnp.maximum(b, 0)
            for h in range(full):
                outs[k][slot, per_block * h:per_block * (h + 1), :] = traces[0, b, :, h * LANES:(h + 1) * LANES]
            notes = jnp.where(lane == tail, jnp.where(live, src[0, b] + 1, 0), 0)
            for i in range(per_block):
                notes = jnp.where(lane == tail + 1 + i, rec[i, b], notes)
            outs[k][slot, per_block * full:per_block * (full + 1), :] = notes.astype(jnp.float32)
            outs[k][slot, per_block * full:per_block * (full + 1), 0:tail] = traces[0, b, :, full * LANES:]


def pack(src, rec, ap, traces, chips, capacity):
    rows = traces.shape[2] * -(-traces.shape[3] // LANES)
    return pl.pallas_call(
        functools.partial(pack_kernel, chips, capacity),
        out_shape=[jax.ShapeDtypeStruct((2 * capacity, rows, LANES), jnp.float32)] * chips,
        in_specs=[SMEM, SMEM, SMEM, VMEM],
        out_specs=[VMEM] * chips,
        scratch_shapes=[pltpu.SMEM((2 * chips * capacity,), jnp.int32), pltpu.SMEM((2 * chips,), jnp.int32)],
        compiler_params=PARAMS,
    )(src, rec, ap, traces)


def triangles(x, lane, per_block):
    zero = jnp.zeros((per_block, LANES), jnp.float32)
    after = jnp.concatenate([x[per_block:], zero], 0)
    before = jnp.concatenate([zero, x[:-per_block]], 0)
    pairs = []
    for k in (1, 2, 3, 4):
        ahead = pltpu.roll(jnp.where(lane < k, after, x), LANES - k, 1)
        behind = pltpu.roll(jnp.where(lane >= LANES - k, before, x), k, 1)
        pairs.append(ahead + behind)
    a, b, c, d = pairs
    return (
        0.5 * x + 0.25 * a,
        (3.0 * x + 2.0 * a + b) * (1.0 / 9.0),
        (5.0 * x + 4.0 * a + 3.0 * b + 2.0 * c + d) * (1.0 / 25.0),
    )


def migrate_kernel(capacity, per_block, samples, arrived, t0, a0, w0, t1, a1, w1, image_in, image, filtered, notes, sem):
    rows = arrived.shape[1]
    note_rows = pl.ds(rows - SUBLANES, SUBLANES)
    copy = pltpu.make_async_copy(arrived.at[:, note_rows, :], notes, sem)
    copy.start()
    lane = lax.broadcasted_iota(jnp.int32, (rows, LANES), 1)
    row = lax.broadcasted_iota(jnp.int32, (rows, LANES), 0)
    full, tail = samples // LANES, samples % LANES
    inside = (row < per_block * full) | (lane < tail)
    steps = rows // per_block
    for slot in range(2 * capacity):
        layers = triangles(jnp.where(inside, arrived[slot], 0.0), lane, per_block)
        for c in range(3):
            filtered[slot, c] = layers[c]
    copy.wait()
    note_row = SUBLANES - per_block
    image[...] = image_in[...]

    for q, (times, amps, widths) in enumerate(((t0, a0, w0), (t1, a1, w1))):
        live = jnp.int32(0)
        for j in range(capacity):
            live = live + (notes[q * capacity + j, note_row, tail] > 0.5).astype(jnp.int32)

        def add_slot(j, _, q=q, times=times, amps=amps, widths=widths):
            slot = q * capacity + j
            s = notes[slot, note_row, tail].astype(jnp.int32) - 1
            for i in range(per_block):
                r = notes[slot, note_row, tail + 1 + i].astype(jnp.int32)
                for half in range(times.shape[1] // SUBLANES):
                    part = pl.ds(SUBLANES * half, SUBLANES)
                    t = times[s, part] + times[r, part]
                    c = jnp.maximum(widths[s, part], widths[r, part])
                    weight = amps[s, part] * amps[r, part]
                    within = t & (LANES - 1)
                    wanted = c * steps + (t >> 7)
                    total = None
                    for c in range(3):
                        for h in range(steps):
                            line = filtered[slot, c, pl.ds(per_block * h + i, 1), :]
                            got = jnp.take_along_axis(
                                jnp.broadcast_to(line, (SUBLANES, LANES)), within, axis=1
                            )
                            total = got if total is None else jnp.where(wanted == c * steps + h, got, total)
                    image[q, part] += weight * total
            return 0

        lax.fori_loop(0, live, add_slot, 0)


def migrate(arrived, own, sibling, image, per_block, samples):
    capacity = arrived.shape[0] // 2
    return pl.pallas_call(
        functools.partial(migrate_kernel, capacity, per_block, samples),
        out_shape=jax.ShapeDtypeStruct(image.shape, jnp.float32),
        in_specs=[VMEM] * 8,
        out_specs=VMEM,
        scratch_shapes=[
            pltpu.VMEM((2 * capacity, 3) + arrived.shape[1:], jnp.float32),
            pltpu.SMEM((2 * capacity, SUBLANES, LANES), jnp.float32),
            pltpu.SemaphoreType.DMA,
        ],
        compiler_params=PARAMS,
        cost_estimate=pl.CostEstimate(flops=20_000_000, bytes_accessed=2_000_000, transcendentals=0),
    )(arrived, *own, *sibling, image)


def slab_kernel(classes, mine, other, *outs):
    me = lax.axis_index("offs")
    depth = outs[0].shape[0]
    whole = mine[0] + other[...]
    image = outs[-1]
    image[...] = whole
    for k in range(classes):
        outs[k][...] = image[pl.ds((me ^ k) * depth, depth), :]


def slabs(mine, other, classes):
    shape = other.shape
    part = jax.ShapeDtypeStruct((shape[0] // classes, shape[1]), jnp.float32)
    return pl.pallas_call(
        functools.partial(slab_kernel, classes),
        out_shape=[part] * classes,
        in_specs=[VMEM] * 2,
        out_specs=[VMEM] * classes,
        scratch_shapes=[pltpu.VMEM(shape, jnp.float32)],
        compiler_params=PARAMS,
    )(mine, other)


def gather_kernel(classes, *refs):
    out = refs[-1]
    me = lax.axis_index("offs")
    depth = out.shape[1]
    for k in range(classes):
        for d in range(depth):
            out[0, d, pl.ds(me ^ k, 1), :] = refs[k][pl.ds(d, 1), :]


def assemble(parts):
    classes = len(parts)
    depth, cells = parts[0].shape
    return pl.pallas_call(
        functools.partial(gather_kernel, classes),
        out_shape=jax.ShapeDtypeStruct((1, depth, classes, cells), jnp.float32),
        in_specs=[VMEM] * classes,
        out_specs=VMEM,
        compiler_params=PARAMS,
    )(*parts)


def swap(value, axis, k):
    size = lax.axis_size(axis)
    return lax.ppermute(value, axis, [(i, i ^ k) for i in range(size)])


def body(traces, src_node, rec_node, aperture, time_table, amp_table, width_table):
    tiles = lax.axis_size("tile")
    classes = lax.axis_size("offs")
    chips = tiles // 2
    blocks, per_block, samples = traces.shape[1:]
    listed = aperture.shape[2]
    capacity = (3 * blocks * listed + 2 * tiles - 1) // (2 * tiles)
    nodes, _, points = time_table.shape
    own = tuple(t.reshape(nodes, points // LANES, LANES) for t in (time_table, amp_table, width_table))

    packed = pack(src_node, rec_node[0].T, aperture[0].T, traces, chips, capacity)
    arrived = [packed[0]] + [swap(packed[k], "tile", 2 * k) for k in range(1, chips)]
    sibling = tuple(swap(t, "tile", 1) for t in own)
    image = jnp.zeros((2, points // LANES, LANES), jnp.float32)
    for k in range(chips):
        image = migrate(arrived[k], own, sibling, image, per_block, samples)
    parts = slabs(image, swap(image[1], "tile", 1), classes)
    return assemble([parts[0]] + [swap(parts[k], "offs", k) for k in range(1, classes)])


def solution(mesh):
    return jax.shard_map(
        body,
        mesh=mesh,
        in_specs=(
            P("offs", "tile", None, None),
            P("offs", "tile"),
            P("offs", "tile", None),
            P("offs", "tile", None),
            P(None, "tile", None),
            P(None, "tile", None),
            P(None, "tile", None),
        ),
        out_specs=P("tile", "offs", None, None),
        check_vma=False,
    )
```

```python
import functools
import math

import jax
import jax.numpy as jnp
from jax import lax
from jax.experimental import pallas as pl
from jax.experimental.pallas import tpu as pltpu
from jax.sharding import PartitionSpec as P

LANES = 128
SUBLANES = 8
VMEM = pl.BlockSpec(memory_space=pltpu.VMEM)
HBM = pl.BlockSpec(memory_space=pltpu.HBM)
HALF_WIDTHS = (1, 2, 4)
PARAMS = pltpu.CompilerParams(vmem_limit_bytes=24 << 20)


def pack_kernel(chips, capacity, src_in, rec_in, ap_in, traces_in, *rest):
    outs = rest[:chips]
    src, rec, ap, traces, block_of, count, sems = rest[chips:]
    copies = [
        pltpu.make_async_copy(a, b, sems.at[n])
        for n, (a, b) in enumerate(((ap_in, ap), (src_in, src), (rec_in, rec)))
    ]
    blocks, per_block, samples = traces.shape
    pieces = sems.shape[0] - 3
    size = blocks // pieces
    for n in range(pieces):
        part = pl.ds(n * size, size)
        copies.append(pltpu.make_async_copy(traces_in.at[0, part], traces.at[part], sems.at[3 + n]))
    for copy in copies:
        copy.start()
    listed = ap.shape[0]
    me = lax.axis_index("tile")
    z, core = me >> 1, me & 1
    for n in range(2 * chips):
        count[n] = 0
    for n in range(2 * chips * capacity):
        block_of[n] = -1
    copies[0].wait()
    for b in range(blocks):
        for e in range(listed):
            tile = ap[e, b]
            group = ((tile >> 1) ^ z) * 2 + ((tile & 1) ^ core)
            place = count[group]
            count[group] = place + 1
            block_of[group * capacity + place] = b
    for copy in copies[1:]:
        copy.wait()
    full, tail = samples // LANES, samples % LANES
    lane = lax.broadcasted_iota(jnp.int32, (per_block, LANES), 1)
    for k in range(chips):
        for slot in range(2 * capacity):
            b = block_of[k * 2 * capacity + slot]
            live = b >= 0
            b = jnp.maximum(b, 0)
            for h in range(full):
                outs[k][slot, per_block * h:per_block * (h + 1), :] = traces[b, :, h * LANES:(h + 1) * LANES]
            notes = jnp.where(lane == tail, jnp.where(live, src[0, b] + 1, 0), 0)
            for i in range(per_block):
                notes = jnp.where(lane == tail + 1 + i, rec[i, b], notes)
            outs[k][slot, per_block * full:per_block * (full + 1), :] = notes.astype(jnp.float32)
            outs[k][slot, per_block * full:per_block * (full + 1), 0:tail] = traces[b, :, full * LANES:]


def pack(src, rec, ap, traces, chips, capacity):
    blocks, per_block, samples = traces.shape[1:]
    rows = per_block * -(-samples // LANES)
    pieces = math.gcd(blocks, 4)
    return pl.pallas_call(
        functools.partial(pack_kernel, chips, capacity),
        out_shape=[jax.ShapeDtypeStruct((2 * capacity, rows, LANES), jnp.float32)] * chips,
        in_specs=[HBM] * 4,
        out_specs=[VMEM] * chips,
        scratch_shapes=[
            pltpu.SMEM(src.shape, jnp.int32),
            pltpu.SMEM(rec.shape, jnp.int32),
            pltpu.SMEM(ap.shape, jnp.int32),
            pltpu.VMEM(traces.shape[1:], jnp.float32),
            pltpu.SMEM((2 * chips * capacity,), jnp.int32),
            pltpu.SMEM((2 * chips,), jnp.int32),
            pltpu.SemaphoreType.DMA((3 + pieces,)),
        ],
        compiler_params=PARAMS,
    )(src, rec, ap, traces)


def filter_matrix():
    shape = (2 * LANES, LANES)
    row = lax.broadcasted_iota(jnp.int32, shape, 0)
    column = lax.broadcasted_iota(jnp.int32, shape, 1)
    where = jnp.where(row >= LANES + LANES // 2, row - 2 * LANES, row)
    distance = jnp.abs(where - column)
    return [jnp.maximum(h + 1 - distance, 0).astype(jnp.float32).astype(jnp.bfloat16) for h in HALF_WIDTHS]


def filter_slots(arrived, matrix, filtered, per_block, samples):
    slots, rows, _ = arrived.shape
    lane = lax.broadcasted_iota(jnp.int32, (rows, LANES), 1)
    row = lax.broadcasted_iota(jnp.int32, (rows, LANES), 0)
    inside = (row < per_block * (samples // LANES)) | (lane < samples % LANES)
    zero = jnp.zeros((per_block, LANES), jnp.float32)
    for slot in range(slots):
        x = jnp.where(inside, arrived[slot], 0.0)
        after = jnp.concatenate([x[per_block:], zero], 0)
        before = jnp.concatenate([zero, x[:-per_block]], 0)
        wide = jnp.concatenate([x, jnp.where(lane < LANES // 2, after, before)], 1)
        high = wide.astype(jnp.bfloat16)
        rest = wide - high.astype(jnp.float32)
        middle = rest.astype(jnp.bfloat16)
        low = (rest - middle.astype(jnp.float32)).astype(jnp.bfloat16)
        pieces = jnp.concatenate([high, middle, low], 0)
        for c, h in enumerate(HALF_WIDTHS):
            product = jnp.dot(pieces, matrix[c], preferred_element_type=jnp.float32)
            summed = product[:rows] + (product[rows:2 * rows] + product[2 * rows:])
            filtered[slot, c] = summed * (1.0 / (h + 1) ** 2)


def add_slots(q, capacity, notes, filtered, tables, image, per_block, samples):
    times, amps, widths = tables
    note_row = SUBLANES - per_block
    tail = samples % LANES
    steps = filtered.shape[2] // per_block
    live = jnp.int32(0)
    for j in range(capacity):
        live = live + (notes[q * capacity + j, note_row, tail] > 0.5).astype(jnp.int32)

    def add_slot(j, _):
        slot = q * capacity + j
        s = notes[slot, note_row, tail].astype(jnp.int32) - 1
        for i in range(per_block):
            r = notes[slot, note_row, tail + 1 + i].astype(jnp.int32)
            for half in range(times.shape[1] // SUBLANES):
                part = pl.ds(SUBLANES * half, SUBLANES)
                t = times[s, part] + times[r, part]
                c = jnp.maximum(widths[s, part], widths[r, part])
                weight = amps[s, part] * amps[r, part]
                within = t & (LANES - 1)
                wanted = c * steps + (t >> 7)
                total = None
                for c in range(3):
                    for h in range(steps):
                        line = filtered[slot, c, pl.ds(per_block * h + i, 1), :]
                        got = jnp.take_along_axis(jnp.broadcast_to(line, (SUBLANES, LANES)), within, axis=1)
                        total = got if total is None else jnp.where(wanted == c * steps + h, got, total)
                image[q, part] += weight * total
        return 0

    lax.fori_loop(0, live, add_slot, 0)


def note_copy(arrived, notes, sem):
    part = pl.ds(arrived.shape[1] - SUBLANES, SUBLANES)
    return pltpu.make_async_copy(arrived.at[:, part, :], notes, sem)


def first_kernel(
    capacity, per_block, samples, arrived, own0, own1, own2, sib0, sib1, sib2,
    image, times, amps, widths, matrix, filtered, notes, sems,
):
    pairs = ((own0, times), (own1, amps), (own2, widths))
    loads = []
    pieces = (sems.shape[0] - 1) // 3
    size = times.shape[0] // pieces
    for n, (a, b) in enumerate(pairs):
        for m in range(pieces):
            part = pl.ds(m * size, size)
            loads.append(pltpu.make_async_copy(a.at[part], b.at[part], sems.at[1 + n * pieces + m]))
    copy = note_copy(arrived, notes, sems.at[0])
    copy.start()
    for load in loads:
        load.start()
    layers = filter_matrix()
    for c in range(3):
        matrix[c] = layers[c]
    filter_slots(arrived, matrix, filtered, per_block, samples)
    image[...] = jnp.zeros(image.shape, jnp.float32)
    copy.wait()
    add_slots(1, capacity, notes, filtered, (sib0, sib1, sib2), image, per_block, samples)
    for load in loads:
        load.wait()
    add_slots(0, capacity, notes, filtered, (times, amps, widths), image, per_block, samples)


def next_kernel(
    capacity, per_block, samples, arrived, own0, own1, own2, sib0, sib1, sib2, matrix, image_in,
    image, filtered, notes, sem,
):
    copy = note_copy(arrived, notes, sem)
    copy.start()
    filter_slots(arrived, matrix, filtered, per_block, samples)
    image[...] = image_in[...]
    copy.wait()
    add_slots(1, capacity, notes, filtered, (sib0, sib1, sib2), image, per_block, samples)
    add_slots(0, capacity, notes, filtered, (own0, own1, own2), image, per_block, samples)


COST = pl.CostEstimate(flops=20_000_000, bytes_accessed=2_000_000, transcendentals=0)


def migrate_scratch(arrived):
    slots = arrived.shape[0]
    return [
        pltpu.VMEM((slots, 3) + arrived.shape[1:], jnp.float32),
        pltpu.SMEM((slots, SUBLANES, LANES), jnp.float32),
    ]


def migrate_first(arrived, own, sibling, per_block, samples):
    pieces = math.gcd(own[0].shape[0], 4)
    shape = own[0].shape
    outs = pl.pallas_call(
        functools.partial(first_kernel, arrived.shape[0] // 2, per_block, samples),
        out_shape=[jax.ShapeDtypeStruct((2,) + shape[1:], jnp.float32)]
        + [jax.ShapeDtypeStruct(t.shape, t.dtype) for t in own]
        + [jax.ShapeDtypeStruct((3, 2 * LANES, LANES), jnp.bfloat16)],
        in_specs=[VMEM] + [HBM] * 3 + [VMEM] * 3,
        out_specs=[VMEM] * 5,
        scratch_shapes=migrate_scratch(arrived) + [pltpu.SemaphoreType.DMA((1 + 3 * pieces,))],
        compiler_params=PARAMS,
        cost_estimate=COST,
    )(arrived, *own, *sibling)
    return outs[0], tuple(outs[1:4]), outs[4]


def migrate(arrived, own, sibling, matrix, image, per_block, samples):
    return pl.pallas_call(
        functools.partial(next_kernel, arrived.shape[0] // 2, per_block, samples),
        out_shape=jax.ShapeDtypeStruct(image.shape, jnp.float32),
        in_specs=[VMEM] * 9,
        out_specs=VMEM,
        scratch_shapes=migrate_scratch(arrived) + [pltpu.SemaphoreType.DMA],
        compiler_params=PARAMS,
        cost_estimate=COST,
    )(arrived, *own, *sibling, matrix, image)


def slab_kernel(classes, mine, other, *outs):
    me = lax.axis_index("offs")
    depth = outs[0].shape[0]
    whole = mine[0] + other[...]
    image = outs[-1]
    image[...] = whole
    for k in range(classes):
        outs[k][...] = image[pl.ds((me ^ k) * depth, depth), :]


def slabs(mine, other, classes):
    shape = other.shape
    part = jax.ShapeDtypeStruct((shape[0] // classes, shape[1]), jnp.float32)
    return pl.pallas_call(
        functools.partial(slab_kernel, classes),
        out_shape=[part] * classes,
        in_specs=[VMEM] * 2,
        out_specs=[VMEM] * classes,
        scratch_shapes=[pltpu.VMEM(shape, jnp.float32)],
        compiler_params=PARAMS,
    )(mine, other)


def gather_kernel(classes, *refs):
    out = refs[-1]
    me = lax.axis_index("offs")
    depth = out.shape[1]
    for k in range(classes):
        for d in range(depth):
            out[0, d, pl.ds(me ^ k, 1), :] = refs[k][pl.ds(d, 1), :]


def assemble(parts):
    classes = len(parts)
    depth, cells = parts[0].shape
    return pl.pallas_call(
        functools.partial(gather_kernel, classes),
        out_shape=jax.ShapeDtypeStruct((1, depth, classes, cells), jnp.float32),
        in_specs=[VMEM] * classes,
        out_specs=VMEM,
        compiler_params=PARAMS,
    )(*parts)


def swap(value, axis, k):
    size = lax.axis_size(axis)
    return lax.ppermute(value, axis, [(i, i ^ k) for i in range(size)])


def body(traces, src_node, rec_node, aperture, time_table, amp_table, width_table):
    tiles = lax.axis_size("tile")
    classes = lax.axis_size("offs")
    chips = tiles // 2
    blocks, per_block, samples = traces.shape[1:]
    listed = aperture.shape[2]
    capacity = (3 * blocks * listed + 2 * tiles - 1) // (2 * tiles)
    nodes, _, points = time_table.shape
    own = tuple(t.reshape(nodes, points // LANES, LANES) for t in (time_table, amp_table, width_table))

    packed = pack(src_node, rec_node[0].T, aperture[0].T, traces, chips, capacity)
    arrived = [packed[0]] + [swap(packed[k], "tile", 2 * k) for k in range(1, chips)]
    sibling = tuple(swap(t, "tile", 1) for t in own)
    image, own, matrix = migrate_first(arrived[0], own, sibling, per_block, samples)
    for k in range(1, chips):
        image = migrate(arrived[k], own, sibling, matrix, image, per_block, samples)
    parts = slabs(image, swap(image[1], "tile", 1), classes)
    moved = {0: parts[0]}
    for k in reversed(range(1, classes)):
        moved[k] = swap(parts[k], "offs", k)
    return assemble([moved[k] for k in range(classes)])


def solution(mesh):
    return jax.shard_map(
        body,
        mesh=mesh,
        in_specs=(
            P("offs", "tile", None, None),
            P("offs", "tile"),
            P("offs", "tile", None),
            P("offs", "tile", None),
            P(None, "tile", None),
            P(None, "tile", None),
            P(None, "tile", None),
        ),
        out_specs=P("tile", "offs", None, None),
        check_vma=False,
    )
```

```python
import functools
import math

import jax
import jax.numpy as jnp
from jax import lax
from jax.experimental import pallas as pl
from jax.experimental.pallas import tpu as pltpu
from jax.sharding import PartitionSpec as P

LANES = 128
SUBLANES = 8
VMEM = pl.BlockSpec(memory_space=pltpu.VMEM)
HBM = pl.BlockSpec(memory_space=pltpu.HBM)
PARAMS = pltpu.CompilerParams(vmem_limit_bytes=24 << 20)


def send_orders(chips):
    far = list(range(2, chips))
    return far[:1] + [1] + far[1:], far[::-1][:1] + [1] + far[::-1][1:]


def swap_chips(value, n, chips):
    orders = send_orders(chips)
    return lax.ppermute(value, "tile", [(i, i ^ (2 * orders[i & 1][n])) for i in range(2 * chips)])


def pack_kernel(chips, capacity, src_in, rec_in, ap_in, traces_in, *rest):
    outs = rest[:chips]
    src, rec, ap, traces, block_of, count, sems = rest[chips:]
    copies = [
        pltpu.make_async_copy(a, b, sems.at[n])
        for n, (a, b) in enumerate(((ap_in, ap), (src_in, src), (rec_in, rec)))
    ]
    blocks, per_block, samples = traces.shape
    pieces = sems.shape[0] - 3
    size = blocks // pieces
    for n in range(pieces):
        part = pl.ds(n * size, size)
        copies.append(pltpu.make_async_copy(traces_in.at[0, part], traces.at[part], sems.at[3 + n]))
    for copy in copies:
        copy.start()
    listed = ap.shape[0]
    me = lax.axis_index("tile")
    z, core = me >> 1, me & 1
    for n in range(2 * chips):
        count[n] = 0
    for n in range(2 * chips * capacity):
        block_of[n] = -1
    copies[0].wait()
    for b in range(blocks):
        for e in range(listed):
            tile = ap[e, b]
            group = ((tile >> 1) ^ z) * 2 + ((tile & 1) ^ core)
            place = count[group]
            count[group] = place + 1
            block_of[group * capacity + place] = b
    for copy in copies[1:]:
        copy.wait()
    full, tail = samples // LANES, samples % LANES
    lane = lax.broadcasted_iota(jnp.int32, (per_block, LANES), 1)
    orders = send_orders(chips)
    for n in range(chips):
        k = 0 if n == 0 else jnp.where(core == 0, orders[0][n - 1], orders[1][n - 1])
        for slot in range(2 * capacity):
            b = block_of[k * 2 * capacity + slot]
            live = b >= 0
            b = jnp.maximum(b, 0)
            for h in range(full):
                outs[n][slot, per_block * h:per_block * (h + 1), :] = traces[b, :, h * LANES:(h + 1) * LANES]
            notes = jnp.where(lane == tail, jnp.where(live, src[0, b] + 1, 0), 0)
            for i in range(per_block):
                notes = jnp.where(lane == tail + 1 + i, rec[i, b], notes)
            outs[n][slot, per_block * full:per_block * (full + 1), :] = notes.astype(jnp.float32)
            outs[n][slot, per_block * full:per_block * (full + 1), 0:tail] = traces[b, :, full * LANES:]


def pack(src, rec, ap, traces, chips, capacity):
    blocks, per_block, samples = traces.shape[1:]
    rows = per_block * -(-samples // LANES)
    pieces = math.gcd(blocks, 4)
    return pl.pallas_call(
        functools.partial(pack_kernel, chips, capacity),
        out_shape=[jax.ShapeDtypeStruct((2 * capacity, rows, LANES), jnp.float32)] * chips,
        in_specs=[HBM] * 4,
        out_specs=[VMEM] * chips,
        scratch_shapes=[
            pltpu.SMEM(src.shape, jnp.int32),
            pltpu.SMEM(rec.shape, jnp.int32),
            pltpu.SMEM(ap.shape, jnp.int32),
            pltpu.VMEM(traces.shape[1:], jnp.float32),
            pltpu.SMEM((2 * chips * capacity,), jnp.int32),
            pltpu.SMEM((2 * chips,), jnp.int32),
            pltpu.SemaphoreType.DMA((3 + pieces,)),
        ],
        compiler_params=PARAMS,
    )(*in_hbm(src, rec, ap, traces))


def slots_of(qs, slots):
    return [q * (slots // 2) + j for q in qs for j in range(slots // 2)]


def triangles(x, lane, per_block):
    zero = jnp.zeros((per_block, LANES), jnp.float32)
    after = jnp.concatenate([x[per_block:], zero], 0)
    before = jnp.concatenate([zero, x[:-per_block]], 0)
    pairs = []
    for k in (1, 2, 3, 4):
        ahead = pltpu.roll(jnp.where(lane < k, after, x), LANES - k, 1)
        behind = pltpu.roll(jnp.where(lane >= LANES - k, before, x), k, 1)
        pairs.append(ahead + behind)
    a, b, c, d = pairs
    return (
        0.5 * x + 0.25 * a,
        (3.0 * x + 2.0 * a + b) * (1.0 / 9.0),
        (5.0 * x + 4.0 * a + 3.0 * b + 2.0 * c + d) * (1.0 / 25.0),
    )


def filter_slots(arrived, filtered, per_block, samples, qs):
    slots, rows, _ = arrived.shape
    lane = lax.broadcasted_iota(jnp.int32, (rows, LANES), 1)
    row = lax.broadcasted_iota(jnp.int32, (rows, LANES), 0)
    inside = (row < per_block * (samples // LANES)) | (lane < samples % LANES)
    for slot in slots_of(qs, slots):
        layers = triangles(jnp.where(inside, arrived[slot], 0.0), lane, per_block)
        for c in range(3):
            filtered[slot, c] = layers[c]


def add_slots(q, notes, filtered, tables, image, per_block, samples):
    times, amps, widths = tables
    steps = filtered.shape[2] // per_block
    each = per_block + 1
    capacity = filtered.shape[0] // 2
    live = jnp.int32(0)
    for j in range(capacity):
        live = live + (notes[(q * capacity + j) * each] > 0).astype(jnp.int32)

    def add_slot(j, _):
        slot = q * capacity + j
        s = notes[slot * each] - 1
        for i in range(per_block):
            r = notes[slot * each + 1 + i]
            for half in range(times.shape[1] // SUBLANES):
                part = pl.ds(SUBLANES * half, SUBLANES)
                t = times[s, part] + times[r, part]
                c = jnp.maximum(widths[s, part], widths[r, part])
                weight = amps[s, part] * amps[r, part]
                within = t & (LANES - 1)
                wanted = c * steps + (t >> 7)
                total = None
                for c in range(3):
                    for h in range(steps):
                        line = filtered[slot, c, pl.ds(per_block * h + i, 1), :]
                        got = jnp.take_along_axis(jnp.broadcast_to(line, (SUBLANES, LANES)), within, axis=1)
                        total = got if total is None else jnp.where(wanted == c * steps + h, got, total)
                image[q, part] += weight * total
        return 0

    lax.fori_loop(0, live, add_slot, 0)


def read_notes(arrived, notes, per_block, samples, qs):
    slots, rows, _ = arrived.shape
    tail = samples % LANES
    for slot in slots_of(qs, slots):
        line = arrived[slot, rows - per_block:rows - per_block + 1, :].astype(jnp.int32)
        for i in range(per_block + 1):
            notes[slot * (per_block + 1) + i] = line[0, tail + i]


def first_kernel(
    qs, per_block, samples, arrived, own0, own1, own2, image, times, amps, widths, filtered, notes, sems,
):
    pairs = ((own0, times), (own1, amps), (own2, widths))
    loads = []
    pieces = sems.shape[0] // 3
    size = times.shape[0] // pieces
    for n, (a, b) in enumerate(pairs):
        for m in range(pieces):
            part = pl.ds(m * size, size)
            loads.append(pltpu.make_async_copy(a.at[part], b.at[part], sems.at[n * pieces + m]))
    for load in loads:
        load.start()
    image[...] = jnp.zeros(image.shape, jnp.float32)
    read_notes(arrived, notes, per_block, samples, qs)
    filter_slots(arrived, filtered, per_block, samples, qs)
    for load in loads:
        load.wait()
    for q in qs:
        add_slots(q, notes, filtered, (times, amps, widths), image, per_block, samples)


def next_kernel(
    qs, per_block, samples, arrived, own0, own1, own2, sib0, sib1, sib2, image_in, image, filtered, notes,
):
    read_notes(arrived, notes, per_block, samples, qs)
    filter_slots(arrived, filtered, per_block, samples, qs)
    image[...] = image_in[...]
    for q in qs:
        add_slots(q, notes, filtered, ((own0, own1, own2), (sib0, sib1, sib2))[q], image, per_block, samples)


COST = pl.CostEstimate(flops=20_000_000, bytes_accessed=2_000_000, transcendentals=0)


def migrate_scratch(arrived, per_block):
    slots = arrived.shape[0]
    return [
        pltpu.VMEM((slots, 3) + arrived.shape[1:], jnp.float32),
        pltpu.SMEM((slots * (per_block + 1),), jnp.int32),
    ]


def in_hbm(*arrays):
    return [pltpu.with_memory_space_constraint(a, pltpu.HBM) for a in arrays]


def migrate_first(arrived, own, qs, per_block, samples):
    pieces = math.gcd(own[0].shape[0], 4)
    shape = own[0].shape
    outs = pl.pallas_call(
        functools.partial(first_kernel, qs, per_block, samples),
        out_shape=[jax.ShapeDtypeStruct((2,) + shape[1:], jnp.float32)]
        + [jax.ShapeDtypeStruct(t.shape, t.dtype) for t in own],
        in_specs=[VMEM] + [HBM] * 3,
        out_specs=[VMEM] * 4,
        scratch_shapes=migrate_scratch(arrived, per_block) + [pltpu.SemaphoreType.DMA((3 * pieces,))],
        compiler_params=PARAMS,
        cost_estimate=COST,
    )(arrived, *in_hbm(*own))
    return outs[0], tuple(outs[1:4])


def migrate(arrived, own, sibling, image, qs, per_block, samples):
    return pl.pallas_call(
        functools.partial(next_kernel, qs, per_block, samples),
        out_shape=jax.ShapeDtypeStruct(image.shape, jnp.float32),
        in_specs=[VMEM] * 8,
        out_specs=VMEM,
        scratch_shapes=migrate_scratch(arrived, per_block),
        compiler_params=PARAMS,
        cost_estimate=COST,
    )(arrived, *own, *sibling, image)


def slab_kernel(classes, mine, other, *outs):
    me = lax.axis_index("offs")
    depth = outs[0].shape[0]
    whole = mine[0] + other[...]
    image = outs[-1]
    image[...] = whole
    for k in range(classes):
        outs[k][...] = image[pl.ds((me ^ k) * depth, depth), :]


def slabs(mine, other, classes):
    shape = other.shape
    part = jax.ShapeDtypeStruct((shape[0] // classes, shape[1]), jnp.float32)
    return pl.pallas_call(
        functools.partial(slab_kernel, classes),
        out_shape=[part] * classes,
        in_specs=[VMEM] * 2,
        out_specs=[VMEM] * classes,
        scratch_shapes=[pltpu.VMEM(shape, jnp.float32)],
        compiler_params=PARAMS,
    )(mine, other)


def gather_kernel(classes, *refs):
    out = refs[-1]
    me = lax.axis_index("offs")
    depth = out.shape[1]
    for k in range(classes):
        for d in range(depth):
            out[0, d, pl.ds(me ^ k, 1), :] = refs[k][pl.ds(d, 1), :]


def assemble(parts):
    classes = len(parts)
    depth, cells = parts[0].shape
    return pl.pallas_call(
        functools.partial(gather_kernel, classes),
        out_shape=jax.ShapeDtypeStruct((1, depth, classes, cells), jnp.float32),
        in_specs=[VMEM] * classes,
        out_specs=VMEM,
        compiler_params=PARAMS,
    )(*parts)


def swap(value, axis, k):
    size = lax.axis_size(axis)
    return lax.ppermute(value, axis, [(i, i ^ k) for i in range(size)])


def body(traces, src_node, rec_node, aperture, time_table, amp_table, width_table):
    tiles = lax.axis_size("tile")
    classes = lax.axis_size("offs")
    chips = tiles // 2
    blocks, per_block, samples = traces.shape[1:]
    listed = aperture.shape[2]
    capacity = (3 * blocks * listed + 2 * tiles - 1) // (2 * tiles)
    nodes, _, points = time_table.shape
    own = tuple(t.reshape(nodes, points // LANES, LANES) for t in (time_table, amp_table, width_table))

    packed = pack(src_node, rec_node[0].T, aperture[0].T, traces, chips, capacity)
    arrived = [packed[0]] + [swap_chips(packed[1 + n], n, chips) for n in range(chips - 1)]
    sibling = tuple(swap(t, "tile", 1) for t in lax.optimization_barrier((own, packed[-1]))[0])
    image, own = migrate_first(arrived[0], own, (0,), per_block, samples)
    image = migrate(arrived[0], own, sibling, image, (1,), per_block, samples)
    image = migrate(arrived[1], own, sibling, image, (1, 0), per_block, samples)
    for k in range(2, chips - 1):
        image = migrate(arrived[k], own, sibling, image, (1, 0), per_block, samples)
    image = migrate(arrived[-1], own, sibling, image, (1,), per_block, samples)
    other = swap(image[1], "tile", 1)
    image = migrate(arrived[-1], own, sibling, image, (0,), per_block, samples)
    parts = slabs(image, other, classes)
    return assemble([parts[0]] + [swap(parts[k], "offs", k) for k in range(1, classes)])


def solution(mesh):
    return jax.shard_map(
        body,
        mesh=mesh,
        in_specs=(
            P("offs", "tile", None, None),
            P("offs", "tile"),
            P("offs", "tile", None),
            P("offs", "tile", None),
            P(None, "tile", None),
            P(None, "tile", None),
            P(None, "tile", None),
        ),
        out_specs=P("tile", "offs", None, None),
        check_vma=False,
    )
```

```python
import functools
import math

import jax
import jax.numpy as jnp
from jax import lax
from jax.experimental import pallas as pl
from jax.experimental.pallas import tpu as pltpu
from jax.sharding import PartitionSpec as P

LANES = 128
SUBLANES = 8
VMEM = pl.BlockSpec(memory_space=pltpu.VMEM)
HBM = pl.BlockSpec(memory_space=pltpu.HBM)
PARAMS = pltpu.CompilerParams(vmem_limit_bytes=24 << 20)


def send_order(chips):
    far = list(range(2, chips))
    return far[:1] + [1] + far[1:]


def swap_chips(value, n, chips):
    return swap(value, "tile", 2 * send_order(chips)[n])


def pack_kernel(chips, capacity, src_in, rec_in, ap_in, traces_in, *rest):
    outs = rest[:chips]
    src, rec, ap, traces, block_of, count, sems = rest[chips:]
    copies = [
        pltpu.make_async_copy(a, b, sems.at[n])
        for n, (a, b) in enumerate(((ap_in, ap), (src_in, src), (rec_in, rec)))
    ]
    blocks, per_block, samples = traces.shape
    pieces = sems.shape[0] - 3
    size = blocks // pieces
    for n in range(pieces):
        part = pl.ds(n * size, size)
        copies.append(pltpu.make_async_copy(traces_in.at[0, part], traces.at[part], sems.at[3 + n]))
    for copy in copies:
        copy.start()
    listed = ap.shape[0]
    me = lax.axis_index("tile")
    z, core = me >> 1, me & 1
    for n in range(2 * chips):
        count[n] = 0
    for n in range(2 * chips * capacity):
        block_of[n] = -1
    copies[0].wait()
    for b in range(blocks):
        for e in range(listed):
            tile = ap[e, b]
            group = ((tile >> 1) ^ z) * 2 + ((tile & 1) ^ core)
            place = count[group]
            count[group] = place + 1
            block_of[group * capacity + place] = b
    for copy in copies[1:]:
        copy.wait()
    full, tail = samples // LANES, samples % LANES
    lane = lax.broadcasted_iota(jnp.int32, (per_block, LANES), 1)
    distances = [0] + send_order(chips)
    for n in range(chips):
        k = distances[n]
        for slot in range(2 * capacity):
            b = block_of[k * 2 * capacity + slot]
            live = b >= 0
            b = jnp.maximum(b, 0)
            for h in range(full):
                outs[n][slot, per_block * h:per_block * (h + 1), :] = traces[b, :, h * LANES:(h + 1) * LANES]
            notes = jnp.where(lane == tail, jnp.where(live, src[0, b] + 1, 0), 0)
            for i in range(per_block):
                notes = jnp.where(lane == tail + 1 + i, rec[i, b], notes)
            outs[n][slot, per_block * full:per_block * (full + 1), :] = notes.astype(jnp.float32)
            outs[n][slot, per_block * full:per_block * (full + 1), 0:tail] = traces[b, :, full * LANES:]


def pack(src, rec, ap, traces, chips, capacity):
    blocks, per_block, samples = traces.shape[1:]
    rows = per_block * -(-samples // LANES)
    pieces = math.gcd(blocks, 4)
    return pl.pallas_call(
        functools.partial(pack_kernel, chips, capacity),
        out_shape=[jax.ShapeDtypeStruct((2 * capacity, rows, LANES), jnp.float32)] * chips,
        in_specs=[HBM] * 4,
        out_specs=[VMEM] * chips,
        scratch_shapes=[
            pltpu.SMEM(src.shape, jnp.int32),
            pltpu.SMEM(rec.shape, jnp.int32),
            pltpu.SMEM(ap.shape, jnp.int32),
            pltpu.VMEM(traces.shape[1:], jnp.float32),
            pltpu.SMEM((2 * chips * capacity,), jnp.int32),
            pltpu.SMEM((2 * chips,), jnp.int32),
            pltpu.SemaphoreType.DMA((3 + pieces,)),
        ],
        compiler_params=PARAMS,
    )(*in_hbm(src, rec, ap, traces))


def slots_of(qs, slots):
    return [q * (slots // 2) + j for q in qs for j in range(slots // 2)]


def triangles(x, lane, per_block):
    zero = jnp.zeros((per_block, LANES), jnp.float32)
    after = jnp.concatenate([x[per_block:], zero], 0)
    before = jnp.concatenate([zero, x[:-per_block]], 0)
    pairs = []
    for k in (1, 2, 3, 4):
        ahead = pltpu.roll(jnp.where(lane < k, after, x), LANES - k, 1)
        behind = pltpu.roll(jnp.where(lane >= LANES - k, before, x), k, 1)
        pairs.append(ahead + behind)
    a, b, c, d = pairs
    return (
        0.5 * x + 0.25 * a,
        (3.0 * x + 2.0 * a + b) * (1.0 / 9.0),
        (5.0 * x + 4.0 * a + 3.0 * b + 2.0 * c + d) * (1.0 / 25.0),
    )


def filter_slots(arrived, filtered, per_block, samples, qs):
    slots, rows, _ = arrived.shape
    lane = lax.broadcasted_iota(jnp.int32, (rows, LANES), 1)
    row = lax.broadcasted_iota(jnp.int32, (rows, LANES), 0)
    inside = (row < per_block * (samples // LANES)) | (lane < samples % LANES)
    for slot in slots_of(qs, slots):
        layers = triangles(jnp.where(inside, arrived[slot], 0.0), lane, per_block)
        for c in range(3):
            filtered[slot, c] = layers[c]


def add_slots(q, notes, filtered, tables, image, per_block, samples):
    times, amps, widths = tables
    steps = filtered.shape[2] // per_block
    each = per_block + 1
    capacity = filtered.shape[0] // 2
    live = jnp.int32(0)
    for j in range(capacity):
        live = live + (notes[(q * capacity + j) * each] > 0).astype(jnp.int32)

    def add_slot(j, _):
        slot = q * capacity + j
        s = notes[slot * each] - 1
        for i in range(per_block):
            r = notes[slot * each + 1 + i]
            for half in range(times.shape[1] // SUBLANES):
                part = pl.ds(SUBLANES * half, SUBLANES)
                t = times[s, part] + times[r, part]
                c = jnp.maximum(widths[s, part], widths[r, part])
                weight = amps[s, part] * amps[r, part]
                within = t & (LANES - 1)
                wanted = c * steps + (t >> 7)
                total = None
                for c in range(3):
                    for h in range(steps):
                        line = filtered[slot, c, pl.ds(per_block * h + i, 1), :]
                        got = jnp.take_along_axis(jnp.broadcast_to(line, (SUBLANES, LANES)), within, axis=1)
                        total = got if total is None else jnp.where(wanted == c * steps + h, got, total)
                image[q, part] += weight * total
        return 0

    lax.fori_loop(0, live, add_slot, 0)


def read_notes(arrived, notes, per_block, samples, qs):
    slots, rows, _ = arrived.shape
    tail = samples % LANES
    for slot in slots_of(qs, slots):
        line = arrived[slot, rows - per_block:rows - per_block + 1, :].astype(jnp.int32)
        for i in range(per_block + 1):
            notes[slot * (per_block + 1) + i] = line[0, tail + i]


def first_kernel(
    qs, per_block, samples, arrived, own0, own1, own2, image, times, amps, widths, filtered, notes, sems,
):
    pairs = ((own0, times), (own1, amps), (own2, widths))
    loads = []
    pieces = sems.shape[0] // 3
    size = times.shape[0] // pieces
    for n, (a, b) in enumerate(pairs):
        for m in range(pieces):
            part = pl.ds(m * size, size)
            loads.append(pltpu.make_async_copy(a.at[part], b.at[part], sems.at[n * pieces + m]))
    for load in loads:
        load.start()
    image[...] = jnp.zeros(image.shape, jnp.float32)
    read_notes(arrived, notes, per_block, samples, qs)
    filter_slots(arrived, filtered, per_block, samples, qs)
    for load in loads:
        load.wait()
    for q in qs:
        add_slots(q, notes, filtered, (times, amps, widths), image, per_block, samples)


def next_kernel(
    qs, per_block, samples, arrived, own0, own1, own2, sib0, sib1, sib2, image_in, image, filtered, notes,
):
    read_notes(arrived, notes, per_block, samples, qs)
    filter_slots(arrived, filtered, per_block, samples, qs)
    image[...] = image_in[...]
    for q in qs:
        add_slots(q, notes, filtered, ((own0, own1, own2), (sib0, sib1, sib2))[q], image, per_block, samples)


COST = pl.CostEstimate(flops=20_000_000, bytes_accessed=2_000_000, transcendentals=0)


def migrate_scratch(arrived, per_block):
    slots = arrived.shape[0]
    return [
        pltpu.VMEM((slots, 3) + arrived.shape[1:], jnp.float32),
        pltpu.SMEM((slots * (per_block + 1),), jnp.int32),
    ]


def in_hbm(*arrays):
    return [pltpu.with_memory_space_constraint(a, pltpu.HBM) for a in arrays]


def migrate_first(arrived, own, qs, per_block, samples):
    pieces = math.gcd(own[0].shape[0], 4)
    shape = own[0].shape
    outs = pl.pallas_call(
        functools.partial(first_kernel, qs, per_block, samples),
        out_shape=[jax.ShapeDtypeStruct((2,) + shape[1:], jnp.float32)]
        + [jax.ShapeDtypeStruct(t.shape, t.dtype) for t in own],
        in_specs=[VMEM] + [HBM] * 3,
        out_specs=[VMEM] * 4,
        scratch_shapes=migrate_scratch(arrived, per_block) + [pltpu.SemaphoreType.DMA((3 * pieces,))],
        compiler_params=PARAMS,
        cost_estimate=COST,
    )(arrived, *in_hbm(*own))
    return outs[0], tuple(outs[1:4])


def migrate(arrived, own, sibling, image, qs, per_block, samples):
    return pl.pallas_call(
        functools.partial(next_kernel, qs, per_block, samples),
        out_shape=jax.ShapeDtypeStruct(image.shape, jnp.float32),
        in_specs=[VMEM] * 8,
        out_specs=VMEM,
        scratch_shapes=migrate_scratch(arrived, per_block),
        compiler_params=PARAMS,
        cost_estimate=COST,
    )(arrived, *own, *sibling, image)


def halve_kernel(distance, counts, *refs):
    ins, (keep, send) = refs[:-2], refs[-2:]
    upper = (lax.axis_index("offs") & distance) != 0
    rows = keep.shape[1]
    at = 0
    for ref, count in zip(ins, counts):
        for j in range(count):
            low, high = ref[j, :rows], ref[j, rows:]
            keep[at] = jnp.where(upper, high, low)
            send[at] = jnp.where(upper, low, high)
            at += 1


def sum_halve_kernel(distance, image, other, keep, send):
    upper = (lax.axis_index("offs") & distance) != 0
    rows = keep.shape[1]
    whole = image[0] + other[...]
    low, high = whole[:rows], whole[rows:]
    keep[0] = jnp.where(upper, high, low)
    send[0] = jnp.where(upper, low, high)


def halve(kernel, arrays, held, rows):
    part = jax.ShapeDtypeStruct((held, rows // 2, LANES), jnp.float32)
    return pl.pallas_call(
        kernel,
        out_shape=[part, part],
        in_specs=[VMEM] * len(arrays),
        out_specs=[VMEM] * 2,
        compiler_params=PARAMS,
    )(*arrays)


def gather_kernel(order, keep, came, out):
    me = lax.axis_index("offs")
    held, depth, _ = keep.shape
    for j, distance in enumerate(order):
        ref, at = (keep, j) if j < held else (came, j - held)
        for d in range(depth):
            out[0, d, pl.ds(me ^ distance, 1), :] = ref[at, pl.ds(d, 1), :]


def exchange_slabs(image, other, classes):
    rows = other.shape[0]
    distance = classes // 2
    keep, send = halve(functools.partial(sum_halve_kernel, distance), (image, other), 1, rows)
    order = [0]
    while True:
        came = swap(send, "offs", distance)
        order = order + [k ^ distance for k in order]
        rows //= 2
        distance //= 2
        if distance == 0:
            break
        counts = (len(order) // 2,) * 2
        keep, send = halve(functools.partial(halve_kernel, distance, counts), (keep, came), len(order), rows)
    return pl.pallas_call(
        functools.partial(gather_kernel, order),
        out_shape=jax.ShapeDtypeStruct((1, rows, classes, LANES), jnp.float32),
        in_specs=[VMEM] * 2,
        out_specs=VMEM,
        compiler_params=PARAMS,
    )(keep, came)


def swap(value, axis, k):
    size = lax.axis_size(axis)
    return lax.ppermute(value, axis, [(i, i ^ k) for i in range(size)])


def body(traces, src_node, rec_node, aperture, time_table, amp_table, width_table):
    tiles = lax.axis_size("tile")
    classes = lax.axis_size("offs")
    chips = tiles // 2
    blocks, per_block, samples = traces.shape[1:]
    listed = aperture.shape[2]
    capacity = (3 * blocks * listed + 2 * tiles - 1) // (2 * tiles)
    nodes, _, points = time_table.shape
    own = tuple(t.reshape(nodes, points // LANES, LANES) for t in (time_table, amp_table, width_table))

    packed = pack(src_node, rec_node[0].T, aperture[0].T, traces, chips, capacity)
    arrived = [packed[0]] + [swap_chips(packed[1 + n], n, chips) for n in range(chips - 1)]
    sibling = tuple(swap(t, "tile", 1) for t in own)
    image, own = migrate_first(arrived[0], own, (0,), per_block, samples)
    image = migrate(arrived[0], own, sibling, image, (1,), per_block, samples)
    image = migrate(arrived[1], own, sibling, image, (1, 0), per_block, samples)
    for k in range(2, chips - 1):
        image = migrate(arrived[k], own, sibling, image, (1, 0), per_block, samples)
    image = migrate(arrived[-1], own, sibling, image, (1,), per_block, samples)
    other = swap(image[1], "tile", 1)
    image = migrate(arrived[-1], own, sibling, image, (0,), per_block, samples)
    return exchange_slabs(image, other, classes)


def solution(mesh):
    return jax.shard_map(
        body,
        mesh=mesh,
        in_specs=(
            P("offs", "tile", None, None),
            P("offs", "tile"),
            P("offs", "tile", None),
            P("offs", "tile", None),
            P(None, "tile", None),
            P(None, "tile", None),
            P(None, "tile", None),
        ),
        out_specs=P("tile", "offs", None, None),
        check_vma=False,
    )
```

```python
import functools
import math

import jax
import jax.numpy as jnp
from jax import lax
from jax.experimental import pallas as pl
from jax.experimental.pallas import tpu as pltpu
from jax.sharding import PartitionSpec as P

LANES = 128
SUBLANES = 8
VMEM = pl.BlockSpec(memory_space=pltpu.VMEM)
HBM = pl.BlockSpec(memory_space=pltpu.HBM)
PARAMS = pltpu.CompilerParams(vmem_limit_bytes=24 << 20)


def send_order(chips):
    far = list(range(2, chips))
    return far[:1] + [1] + far[1:]


def swap_chips(value, n, chips):
    return swap(value, "tile", 2 * send_order(chips)[n])


def pack_kernel(chips, capacity, src_in, rec_in, ap_in, traces_in, *rest):
    outs = rest[:chips]
    src, rec, ap, traces, block_of, count, sems = rest[chips:]
    copies = [
        pltpu.make_async_copy(a, b, sems.at[n])
        for n, (a, b) in enumerate(((ap_in, ap), (src_in, src), (rec_in, rec)))
    ]
    blocks, per_block, samples = traces.shape
    pieces = sems.shape[0] - 3
    size = blocks // pieces
    for n in range(pieces):
        part = pl.ds(n * size, size)
        copies.append(pltpu.make_async_copy(traces_in.at[0, part], traces.at[part], sems.at[3 + n]))
    for copy in copies:
        copy.start()
    listed = ap.shape[0]
    me = lax.axis_index("tile")
    z, core = me >> 1, me & 1
    for n in range(2 * chips):
        count[n] = 0
    for n in range(2 * chips * capacity):
        block_of[n] = -1
    copies[0].wait()
    for b in range(blocks):
        for e in range(listed):
            tile = ap[e, b]
            group = ((tile >> 1) ^ z) * 2 + ((tile & 1) ^ core)
            place = count[group]
            count[group] = place + 1
            block_of[group * capacity + place] = b
    for copy in copies[1:]:
        copy.wait()
    full, tail = samples // LANES, samples % LANES
    lane = lax.broadcasted_iota(jnp.int32, (per_block, LANES), 1)
    distances = [0] + send_order(chips)
    for n in range(chips):
        k = distances[n]
        for slot in range(2 * capacity):
            b = block_of[k * 2 * capacity + slot]
            live = b >= 0
            b = jnp.maximum(b, 0)
            for h in range(full):
                outs[n][slot, per_block * h:per_block * (h + 1), :] = traces[b, :, h * LANES:(h + 1) * LANES]
            notes = jnp.where(lane == tail, jnp.where(live, src[0, b] + 1, 0), 0)
            for i in range(per_block):
                notes = jnp.where(lane == tail + 1 + i, rec[i, b], notes)
            outs[n][slot, per_block * full:per_block * (full + 1), :] = notes.astype(jnp.float32)
            outs[n][slot, per_block * full:per_block * (full + 1), 0:tail] = traces[b, :, full * LANES:]


def pack(src, rec, ap, traces, chips, capacity):
    blocks, per_block, samples = traces.shape[1:]
    rows = per_block * -(-samples // LANES)
    pieces = math.gcd(blocks, 4)
    return pl.pallas_call(
        functools.partial(pack_kernel, chips, capacity),
        out_shape=[jax.ShapeDtypeStruct((2 * capacity, rows, LANES), jnp.float32)] * chips,
        in_specs=[HBM] * 4,
        out_specs=[VMEM] * chips,
        scratch_shapes=[
            pltpu.SMEM(src.shape, jnp.int32),
            pltpu.SMEM(rec.shape, jnp.int32),
            pltpu.SMEM(ap.shape, jnp.int32),
            pltpu.VMEM(traces.shape[1:], jnp.float32),
            pltpu.SMEM((2 * chips * capacity,), jnp.int32),
            pltpu.SMEM((2 * chips,), jnp.int32),
            pltpu.SemaphoreType.DMA((3 + pieces,)),
        ],
        compiler_params=PARAMS,
    )(*in_hbm(src, rec, ap, traces))


def slots_of(qs, slots):
    return [q * (slots // 2) + j for q in qs for j in range(slots // 2)]


def triangles(x, lane, per_block):
    zero = jnp.zeros((per_block, LANES), jnp.float32)
    after = jnp.concatenate([x[per_block:], zero], 0)
    before = jnp.concatenate([zero, x[:-per_block]], 0)
    pairs = []
    for k in (1, 2, 3, 4):
        ahead = pltpu.roll(jnp.where(lane < k, after, x), LANES - k, 1)
        behind = pltpu.roll(jnp.where(lane >= LANES - k, before, x), k, 1)
        pairs.append(ahead + behind)
    a, b, c, d = pairs
    return (
        0.5 * x + 0.25 * a,
        (3.0 * x + 2.0 * a + b) * (1.0 / 9.0),
        (5.0 * x + 4.0 * a + 3.0 * b + 2.0 * c + d) * (1.0 / 25.0),
    )


def filter_slots(arrived, filtered, per_block, samples, qs):
    slots, rows, _ = arrived.shape
    lane = lax.broadcasted_iota(jnp.int32, (rows, LANES), 1)
    row = lax.broadcasted_iota(jnp.int32, (rows, LANES), 0)
    inside = (row < per_block * (samples // LANES)) | (lane < samples % LANES)
    for slot in slots_of(qs, slots):
        layers = triangles(jnp.where(inside, arrived[slot], 0.0), lane, per_block)
        for c in range(3):
            filtered[slot, c] = layers[c]


def add_slots(q, notes, filtered, tables, image, per_block, samples):
    times, amps, widths = tables
    steps = filtered.shape[2] // per_block
    each = per_block + 1
    capacity = filtered.shape[0] // 2
    live = jnp.int32(0)
    for j in range(capacity):
        live = live + (notes[(q * capacity + j) * each] > 0).astype(jnp.int32)

    def contribution(slot, part):
        total = None
        s = notes[slot * each] - 1
        for i in range(per_block):
            r = notes[slot * each + 1 + i]
            t = times[s, part] + times[r, part]
            c = jnp.maximum(widths[s, part], widths[r, part])
            weight = amps[s, part] * amps[r, part]
            within = t & (LANES - 1)
            wanted = c * steps + (t >> 7)
            picked = None
            for c in range(3):
                for h in range(steps):
                    line = filtered[slot, c, pl.ds(per_block * h + i, 1), :]
                    got = jnp.take_along_axis(jnp.broadcast_to(line, (SUBLANES, LANES)), within, axis=1)
                    picked = got if picked is None else jnp.where(wanted == c * steps + h, got, picked)
            total = weight * picked if total is None else total + weight * picked
        return total

    def add(slots):
        for half in range(times.shape[1] // SUBLANES):
            part = pl.ds(SUBLANES * half, SUBLANES)
            image[q, part] += sum(contribution(slot, part) for slot in slots)

    def add_two(j, _):
        add((q * capacity + 2 * j, q * capacity + 2 * j + 1))
        return 0

    def add_last(j, _):
        add((q * capacity + j,))
        return 0

    lax.fori_loop(0, live >> 1, add_two, 0)
    lax.fori_loop(live & -2, live, add_last, 0)


def read_notes(arrived, notes, per_block, samples, qs):
    slots, rows, _ = arrived.shape
    tail = samples % LANES
    for slot in slots_of(qs, slots):
        line = arrived[slot, rows - per_block:rows - per_block + 1, :].astype(jnp.int32)
        for i in range(per_block + 1):
            notes[slot * (per_block + 1) + i] = line[0, tail + i]


def first_kernel(
    qs, per_block, samples, arrived, own0, own1, own2, sib0, sib1, sib2, image, times, amps, widths, filtered, notes, sems,
):
    pairs = ((own0, times), (own1, amps), (own2, widths))
    loads = []
    pieces = sems.shape[0] // 3
    size = times.shape[0] // pieces
    for n, (a, b) in enumerate(pairs):
        for m in range(pieces):
            part = pl.ds(m * size, size)
            loads.append(pltpu.make_async_copy(a.at[part], b.at[part], sems.at[n * pieces + m]))
    for load in loads:
        load.start()
    image[...] = jnp.zeros(image.shape, jnp.float32)
    read_notes(arrived, notes, per_block, samples, qs)
    filter_slots(arrived, filtered, per_block, samples, qs)
    add_slots(1, notes, filtered, (sib0, sib1, sib2), image, per_block, samples)
    for load in loads:
        load.wait()
    add_slots(0, notes, filtered, (times, amps, widths), image, per_block, samples)


def next_kernel(
    qs, per_block, samples, arrived, own0, own1, own2, sib0, sib1, sib2, image_in, image, filtered, notes,
):
    read_notes(arrived, notes, per_block, samples, qs)
    filter_slots(arrived, filtered, per_block, samples, qs)
    image[...] = image_in[...]
    for q in qs:
        add_slots(q, notes, filtered, ((own0, own1, own2), (sib0, sib1, sib2))[q], image, per_block, samples)


COST = pl.CostEstimate(flops=20_000_000, bytes_accessed=2_000_000, transcendentals=0)


def migrate_scratch(arrived, per_block):
    slots = arrived.shape[0]
    return [
        pltpu.VMEM((slots, 3) + arrived.shape[1:], jnp.float32),
        pltpu.SMEM((slots * (per_block + 1),), jnp.int32),
    ]


def in_hbm(*arrays):
    return [pltpu.with_memory_space_constraint(a, pltpu.HBM) for a in arrays]


def migrate_first(arrived, own, sibling, per_block, samples):
    pieces = math.gcd(own[0].shape[0], 4)
    shape = own[0].shape
    outs = pl.pallas_call(
        functools.partial(first_kernel, (1, 0), per_block, samples),
        out_shape=[jax.ShapeDtypeStruct((2,) + shape[1:], jnp.float32)]
        + [jax.ShapeDtypeStruct(t.shape, t.dtype) for t in own],
        in_specs=[VMEM] + [HBM] * 3 + [VMEM] * 3,
        out_specs=[VMEM] * 4,
        scratch_shapes=migrate_scratch(arrived, per_block) + [pltpu.SemaphoreType.DMA((3 * pieces,))],
        compiler_params=PARAMS,
        cost_estimate=COST,
    )(arrived, *in_hbm(*own), *sibling)
    return outs[0], tuple(outs[1:4])


def migrate(arrived, own, sibling, image, qs, per_block, samples):
    return pl.pallas_call(
        functools.partial(next_kernel, qs, per_block, samples),
        out_shape=jax.ShapeDtypeStruct(image.shape, jnp.float32),
        in_specs=[VMEM] * 8,
        out_specs=VMEM,
        scratch_shapes=migrate_scratch(arrived, per_block),
        compiler_params=PARAMS,
        cost_estimate=COST,
    )(arrived, *own, *sibling, image)


def halve_kernel(distance, counts, *refs):
    ins, (keep, send) = refs[:-2], refs[-2:]
    upper = (lax.axis_index("offs") & distance) != 0
    rows = keep.shape[1]
    at = 0
    for ref, count in zip(ins, counts):
        for j in range(count):
            low, high = ref[j, :rows], ref[j, rows:]
            keep[at] = jnp.where(upper, high, low)
            send[at] = jnp.where(upper, low, high)
            at += 1


def sum_halve_kernel(distance, image, other, keep, send):
    upper = (lax.axis_index("offs") & distance) != 0
    rows = keep.shape[1]
    whole = image[0] + other[...]
    low, high = whole[:rows], whole[rows:]
    keep[0] = jnp.where(upper, high, low)
    send[0] = jnp.where(upper, low, high)


def halve(kernel, arrays, held, rows):
    part = jax.ShapeDtypeStruct((held, rows // 2, LANES), jnp.float32)
    return pl.pallas_call(
        kernel,
        out_shape=[part, part],
        in_specs=[VMEM] * len(arrays),
        out_specs=[VMEM] * 2,
        compiler_params=PARAMS,
    )(*arrays)


def gather_kernel(order, keep, came, out):
    me = lax.axis_index("offs")
    held, depth, _ = keep.shape
    for j, distance in enumerate(order):
        ref, at = (keep, j) if j < held else (came, j - held)
        for d in range(depth):
            out[0, d, pl.ds(me ^ distance, 1), :] = ref[at, pl.ds(d, 1), :]


def exchange_slabs(image, other, classes):
    rows = other.shape[0]
    distance = classes // 2
    keep, send = halve(functools.partial(sum_halve_kernel, distance), (image, other), 1, rows)
    order = [0]
    while True:
        came = swap(send, "offs", distance)
        order = order + [k ^ distance for k in order]
        rows //= 2
        distance //= 2
        if distance == 0:
            break
        counts = (len(order) // 2,) * 2
        keep, send = halve(functools.partial(halve_kernel, distance, counts), (keep, came), len(order), rows)
    return pl.pallas_call(
        functools.partial(gather_kernel, order),
        out_shape=jax.ShapeDtypeStruct((1, rows, classes, LANES), jnp.float32),
        in_specs=[VMEM] * 2,
        out_specs=VMEM,
        compiler_params=PARAMS,
    )(keep, came)


def swap(value, axis, k):
    size = lax.axis_size(axis)
    return lax.ppermute(value, axis, [(i, i ^ k) for i in range(size)])


def body(traces, src_node, rec_node, aperture, time_table, amp_table, width_table):
    tiles = lax.axis_size("tile")
    classes = lax.axis_size("offs")
    chips = tiles // 2
    blocks, per_block, samples = traces.shape[1:]
    listed = aperture.shape[2]
    capacity = (3 * blocks * listed + 2 * tiles - 1) // (2 * tiles)
    nodes, _, points = time_table.shape
    own = tuple(t.reshape(nodes, points // LANES, LANES) for t in (time_table, amp_table, width_table))

    packed = pack(src_node, rec_node[0].T, aperture[0].T, traces, chips, capacity)
    arrived = [packed[0]] + [swap_chips(packed[1 + n], n, chips) for n in range(chips - 1)]
    sibling = tuple(swap(t, "tile", 1) for t in own)
    image, own = migrate_first(arrived[0], own, sibling, per_block, samples)
    image = migrate(arrived[1], own, sibling, image, (1, 0), per_block, samples)
    for k in range(2, chips - 1):
        image = migrate(arrived[k], own, sibling, image, (1, 0), per_block, samples)
    image = migrate(arrived[-1], own, sibling, image, (1,), per_block, samples)
    other = swap(image[1], "tile", 1)
    image = migrate(arrived[-1], own, sibling, image, (0,), per_block, samples)
    return exchange_slabs(image, other, classes)


def solution(mesh):
    return jax.shard_map(
        body,
        mesh=mesh,
        in_specs=(
            P("offs", "tile", None, None),
            P("offs", "tile"),
            P("offs", "tile", None),
            P("offs", "tile", None),
            P(None, "tile", None),
            P(None, "tile", None),
            P(None, "tile", None),
        ),
        out_specs=P("tile", "offs", None, None),
        check_vma=False,
    )
```

```python
import functools
import math

import jax
import jax.numpy as jnp
from jax import lax
from jax.experimental import pallas as pl
from jax.experimental.pallas import tpu as pltpu
from jax.sharding import PartitionSpec as P

LANES = 128
SUBLANES = 8
VMEM = pl.BlockSpec(memory_space=pltpu.VMEM)
HBM = pl.BlockSpec(memory_space=pltpu.HBM)
PARAMS = pltpu.CompilerParams(vmem_limit_bytes=24 << 20)


def send_order(chips):
    far = list(range(2, chips))
    return far[:1] + [1] + far[1:]


def swap_chips(value, n, chips):
    return swap(value, "tile", 2 * send_order(chips)[n])


def pack_kernel(chips, capacity, src_in, rec_in, ap_in, traces_in, *rest):
    outs = rest[:chips]
    src, rec, ap, traces, block_of, count, sems = rest[chips:]
    copies = [
        pltpu.make_async_copy(a, b, sems.at[n])
        for n, (a, b) in enumerate(((ap_in, ap), (src_in, src), (rec_in, rec)))
    ]
    blocks, per_block, samples = traces.shape
    pieces = sems.shape[0] - 3
    size = blocks // pieces
    for n in range(pieces):
        part = pl.ds(n * size, size)
        copies.append(pltpu.make_async_copy(traces_in.at[0, part], traces.at[part], sems.at[3 + n]))
    for copy in copies:
        copy.start()
    listed = ap.shape[0]
    me = lax.axis_index("tile")
    z, core = me >> 1, me & 1
    for n in range(2 * chips):
        count[n] = 0
    for n in range(2 * chips * capacity):
        block_of[n] = -1
    copies[0].wait()
    for b in range(blocks):
        for e in range(listed):
            tile = ap[e, b]
            group = ((tile >> 1) ^ z) * 2 + ((tile & 1) ^ core)
            place = count[group]
            count[group] = place + 1
            block_of[group * capacity + place] = b
    for copy in copies[1:]:
        copy.wait()
    full, tail = samples // LANES, samples % LANES
    lane = lax.broadcasted_iota(jnp.int32, (per_block, LANES), 1)
    distances = [0] + send_order(chips)
    for n in range(chips):
        k = distances[n]
        for slot in range(2 * capacity):
            b = block_of[k * 2 * capacity + slot]
            live = b >= 0
            b = jnp.maximum(b, 0)
            for h in range(full):
                outs[n][slot, per_block * h:per_block * (h + 1), :] = traces[b, :, h * LANES:(h + 1) * LANES]
            notes = jnp.where(lane == tail, jnp.where(live, src[0, b] + 1, 0), 0)
            for i in range(per_block):
                notes = jnp.where(lane == tail + 1 + i, rec[i, b], notes)
            outs[n][slot, per_block * full:per_block * (full + 1), :] = notes.astype(jnp.float32)
            outs[n][slot, per_block * full:per_block * (full + 1), 0:tail] = traces[b, :, full * LANES:]


def pack(src, rec, ap, traces, chips, capacity):
    blocks, per_block, samples = traces.shape[1:]
    rows = per_block * -(-samples // LANES)
    pieces = math.gcd(blocks, 4)
    return pl.pallas_call(
        functools.partial(pack_kernel, chips, capacity),
        out_shape=[jax.ShapeDtypeStruct((2 * capacity, rows, LANES), jnp.float32)] * chips,
        in_specs=[HBM] * 4,
        out_specs=[VMEM] * chips,
        scratch_shapes=[
            pltpu.SMEM(src.shape, jnp.int32),
            pltpu.SMEM(rec.shape, jnp.int32),
            pltpu.SMEM(ap.shape, jnp.int32),
            pltpu.VMEM(traces.shape[1:], jnp.float32),
            pltpu.SMEM((2 * chips * capacity,), jnp.int32),
            pltpu.SMEM((2 * chips,), jnp.int32),
            pltpu.SemaphoreType.DMA((3 + pieces,)),
        ],
        compiler_params=PARAMS,
    )(*in_hbm(src, rec, ap, traces))


def slots_of(qs, slots):
    return [q * (slots // 2) + j for q in qs for j in range(slots // 2)]


def triangles(x, lane, per_block):
    zero = jnp.zeros((per_block, LANES), jnp.float32)
    after = jnp.concatenate([x[per_block:], zero], 0)
    before = jnp.concatenate([zero, x[:-per_block]], 0)
    pairs = []
    for k in (1, 2, 3, 4):
        ahead = pltpu.roll(jnp.where(lane < k, after, x), LANES - k, 1)
        behind = pltpu.roll(jnp.where(lane >= LANES - k, before, x), k, 1)
        pairs.append(ahead + behind)
    a, b, c, d = pairs
    return (
        0.5 * x + 0.25 * a,
        (3.0 * x + 2.0 * a + b) * (1.0 / 9.0),
        (5.0 * x + 4.0 * a + 3.0 * b + 2.0 * c + d) * (1.0 / 25.0),
    )


def filter_slots(arrived, filtered, per_block, samples, qs):
    slots, rows, _ = arrived.shape
    lane = lax.broadcasted_iota(jnp.int32, (rows, LANES), 1)
    row = lax.broadcasted_iota(jnp.int32, (rows, LANES), 0)
    inside = (row < per_block * (samples // LANES)) | (lane < samples % LANES)
    for slot in slots_of(qs, slots):
        layers = triangles(jnp.where(inside, arrived[slot], 0.0), lane, per_block)
        for c in range(3):
            filtered[slot, c] = layers[c]


def add_slots(q, notes, filtered, tables, image, per_block, samples):
    times, amps, widths = tables
    steps = filtered.shape[2] // per_block
    each = per_block + 1
    capacity = filtered.shape[0] // 2
    live = jnp.int32(0)
    for j in range(capacity):
        live = live + (notes[(q * capacity + j) * each] > 0).astype(jnp.int32)

    def contribution(slot, part):
        total = None
        s = notes[slot * each] - 1
        for i in range(per_block):
            r = notes[slot * each + 1 + i]
            t = times[s, part] + times[r, part]
            c = jnp.maximum(widths[s, part], widths[r, part])
            weight = amps[s, part] * amps[r, part]
            within = t & (LANES - 1)
            wanted = c * steps + (t >> 7)
            picked = None
            for c in range(3):
                for h in range(steps):
                    line = filtered[slot, c, pl.ds(per_block * h + i, 1), :]
                    got = jnp.take_along_axis(jnp.broadcast_to(line, (SUBLANES, LANES)), within, axis=1)
                    picked = got if picked is None else jnp.where(wanted == c * steps + h, got, picked)
            total = weight * picked if total is None else total + weight * picked
        return total

    def add(slots):
        for half in range(times.shape[1] // SUBLANES):
            part = pl.ds(SUBLANES * half, SUBLANES)
            image[q, part] += sum(contribution(slot, part) for slot in slots)

    def add_all(j, _):
        add([q * capacity + n for n in range(capacity)])
        return 0

    def add_one(j, _):
        add((q * capacity + j,))
        return 0

    full = (live == capacity).astype(jnp.int32)
    lax.fori_loop(0, full, add_all, 0)
    lax.fori_loop(full * live, live, add_one, 0)


def read_notes(arrived, notes, per_block, samples, qs):
    slots, rows, _ = arrived.shape
    tail = samples % LANES
    for slot in slots_of(qs, slots):
        line = arrived[slot, rows - per_block:rows - per_block + 1, :].astype(jnp.int32)
        for i in range(per_block + 1):
            notes[slot * (per_block + 1) + i] = line[0, tail + i]


def first_kernel(
    qs, per_block, samples, arrived, own0, own1, own2, sib0, sib1, sib2, image, times, amps, widths, filtered, notes, sems,
):
    pairs = ((own0, times), (own1, amps), (own2, widths))
    loads = []
    pieces = sems.shape[0] // 3
    size = times.shape[0] // pieces
    for n, (a, b) in enumerate(pairs):
        for m in range(pieces):
            part = pl.ds(m * size, size)
            loads.append(pltpu.make_async_copy(a.at[part], b.at[part], sems.at[n * pieces + m]))
    for load in loads:
        load.start()
    image[...] = jnp.zeros(image.shape, jnp.float32)
    read_notes(arrived, notes, per_block, samples, qs)
    filter_slots(arrived, filtered, per_block, samples, qs)
    add_slots(1, notes, filtered, (sib0, sib1, sib2), image, per_block, samples)
    for load in loads:
        load.wait()
    add_slots(0, notes, filtered, (times, amps, widths), image, per_block, samples)


def next_kernel(
    qs, per_block, samples, arrived, own0, own1, own2, sib0, sib1, sib2, image_in, image, filtered, notes,
):
    read_notes(arrived, notes, per_block, samples, qs)
    filter_slots(arrived, filtered, per_block, samples, qs)
    image[...] = image_in[...]
    for q in qs:
        add_slots(q, notes, filtered, ((own0, own1, own2), (sib0, sib1, sib2))[q], image, per_block, samples)


COST = pl.CostEstimate(flops=20_000_000, bytes_accessed=2_000_000, transcendentals=0)


def migrate_scratch(arrived, per_block):
    slots = arrived.shape[0]
    return [
        pltpu.VMEM((slots, 3) + arrived.shape[1:], jnp.float32),
        pltpu.SMEM((slots * (per_block + 1),), jnp.int32),
    ]


def in_hbm(*arrays):
    return [pltpu.with_memory_space_constraint(a, pltpu.HBM) for a in arrays]


def migrate_first(arrived, own, sibling, per_block, samples):
    pieces = math.gcd(own[0].shape[0], 4)
    shape = own[0].shape
    outs = pl.pallas_call(
        functools.partial(first_kernel, (1, 0), per_block, samples),
        out_shape=[jax.ShapeDtypeStruct((2,) + shape[1:], jnp.float32)]
        + [jax.ShapeDtypeStruct(t.shape, t.dtype) for t in own],
        in_specs=[VMEM] + [HBM] * 3 + [VMEM] * 3,
        out_specs=[VMEM] * 4,
        scratch_shapes=migrate_scratch(arrived, per_block) + [pltpu.SemaphoreType.DMA((3 * pieces,))],
        compiler_params=PARAMS,
        cost_estimate=COST,
    )(arrived, *in_hbm(*own), *sibling)
    return outs[0], tuple(outs[1:4])


def migrate(arrived, own, sibling, image, qs, per_block, samples):
    return pl.pallas_call(
        functools.partial(next_kernel, qs, per_block, samples),
        out_shape=jax.ShapeDtypeStruct(image.shape, jnp.float32),
        in_specs=[VMEM] * 8,
        out_specs=VMEM,
        scratch_shapes=migrate_scratch(arrived, per_block),
        compiler_params=PARAMS,
        cost_estimate=COST,
    )(arrived, *own, *sibling, image)


def halve_kernel(distance, counts, *refs):
    ins, (keep, send) = refs[:-2], refs[-2:]
    upper = (lax.axis_index("offs") & distance) != 0
    rows = keep.shape[1]
    at = 0
    for ref, count in zip(ins, counts):
        for j in range(count):
            low, high = ref[j, :rows], ref[j, rows:]
            keep[at] = jnp.where(upper, high, low)
            send[at] = jnp.where(upper, low, high)
            at += 1


def sum_halve_kernel(distance, image, other, keep, send):
    upper = (lax.axis_index("offs") & distance) != 0
    rows = keep.shape[1]
    whole = image[0] + other[...]
    low, high = whole[:rows], whole[rows:]
    keep[0] = jnp.where(upper, high, low)
    send[0] = jnp.where(upper, low, high)


def halve(kernel, arrays, held, rows):
    part = jax.ShapeDtypeStruct((held, rows // 2, LANES), jnp.float32)
    return pl.pallas_call(
        kernel,
        out_shape=[part, part],
        in_specs=[VMEM] * len(arrays),
        out_specs=[VMEM] * 2,
        compiler_params=PARAMS,
    )(*arrays)


def gather_kernel(order, keep, came, out):
    me = lax.axis_index("offs")
    held, depth, _ = keep.shape
    for j, distance in enumerate(order):
        ref, at = (keep, j) if j < held else (came, j - held)
        for d in range(depth):
            out[0, d, pl.ds(me ^ distance, 1), :] = ref[at, pl.ds(d, 1), :]


def exchange_slabs(image, other, classes):
    rows = other.shape[0]
    distance = classes // 2
    keep, send = halve(functools.partial(sum_halve_kernel, distance), (image, other), 1, rows)
    order = [0]
    while True:
        came = swap(send, "offs", distance)
        order = order + [k ^ distance for k in order]
        rows //= 2
        distance //= 2
        if distance == 0:
            break
        counts = (len(order) // 2,) * 2
        keep, send = halve(functools.partial(halve_kernel, distance, counts), (keep, came), len(order), rows)
    return pl.pallas_call(
        functools.partial(gather_kernel, order),
        out_shape=jax.ShapeDtypeStruct((1, rows, classes, LANES), jnp.float32),
        in_specs=[VMEM] * 2,
        out_specs=VMEM,
        compiler_params=PARAMS,
    )(keep, came)


def swap(value, axis, k):
    size = lax.axis_size(axis)
    return lax.ppermute(value, axis, [(i, i ^ k) for i in range(size)])


def body(traces, src_node, rec_node, aperture, time_table, amp_table, width_table):
    tiles = lax.axis_size("tile")
    classes = lax.axis_size("offs")
    chips = tiles // 2
    blocks, per_block, samples = traces.shape[1:]
    listed = aperture.shape[2]
    capacity = (3 * blocks * listed + 2 * tiles - 1) // (2 * tiles)
    nodes, _, points = time_table.shape
    own = tuple(t.reshape(nodes, points // LANES, LANES) for t in (time_table, amp_table, width_table))

    packed = pack(src_node, rec_node[0].T, aperture[0].T, traces, chips, capacity)
    arrived = [packed[0]] + [swap_chips(packed[1 + n], n, chips) for n in range(chips - 1)]
    sibling = tuple(swap(t, "tile", 1) for t in own)
    image, own = migrate_first(arrived[0], own, sibling, per_block, samples)
    image = migrate(arrived[1], own, sibling, image, (1, 0), per_block, samples)
    for k in range(2, chips - 1):
        image = migrate(arrived[k], own, sibling, image, (1, 0), per_block, samples)
    image = migrate(arrived[-1], own, sibling, image, (1,), per_block, samples)
    other = swap(image[1], "tile", 1)
    image = migrate(arrived[-1], own, sibling, image, (0,), per_block, samples)
    return exchange_slabs(image, other, classes)


def solution(mesh):
    return jax.shard_map(
        body,
        mesh=mesh,
        in_specs=(
            P("offs", "tile", None, None),
            P("offs", "tile"),
            P("offs", "tile", None),
            P("offs", "tile", None),
            P(None, "tile", None),
            P(None, "tile", None),
            P(None, "tile", None),
        ),
        out_specs=P("tile", "offs", None, None),
        check_vma=False,
    )
```
